32 devices in a mesh: dp: 8 (over z, core), tensor: 4 (over y, x).
Axes of the slice: x: 2, y: 2, z: 4, core: 2. Of those that a mesh axis runs over, the one named last changes fastest.
Arguments:
- inputs: bfloat16 [6144, 4096], P(('dp', 'tensor')), may hold values from -6 to 6
- cotangent: bfloat16 [6144, 4096], P(('dp', 'tensor')), may hold values from -6 to 6
- gate_pre: bfloat16 [6144, 14336], P('dp', 'tensor'), may hold values from -8 to 8
- up_pre: bfloat16 [6144, 14336], P('dp', 'tensor'), may hold values from -6 to 6
- w_down: bfloat16 [14336, 4096], P('tensor', 'dp'), may hold values from -0.046875 to 0.046875
- proj_model: bfloat16 [4096, 128], replicated, may hold values from -0.09375 to 0.09375
- proj_hidden: bfloat16 [14336, 128], P('tensor'), may hold values from -0.046875 to 0.046875
- queries: bfloat16 [256, 8192], P('tensor', 'dp'), may hold values from -0.125 to 0.125
- lengths: int32 [24], P('dp'), may hold values from 1 to 256, as said below
Outputs:
- scores: float32 [24, 256], P('dp', 'tensor')
The draws below stay inside these ranges and needn't reach their ends.
Inputs may be any that keep to these rules, and one draw needn't show every extreme that they name: `lengths`: a route's real tokens fill its first slots, the rest are padding; some route has 256 and some route 1.
All inputs are finite; a program needn't handle non-finite values.
Results may differ from the reference program's by a relative error of at most 0.003.
Values may be sent and summed in bfloat16 or wider, within the bound.
A program may use at most 128 MiB of HBM per device.

```python
import math
import jax
import jax.numpy as jnp
from jax import lax

D = 4096
FF = 14336
RANK = 64
QUERIES = 256
LEN = 256
ROUTES = 24
TOKENS = 6144
FEATURES = 8192


def draw_lengths(key, part):
    key = jax.random.fold_in(key, 7)
    first_key, second_key = jax.random.split(key)
    values = jax.random.randint(first_key, (ROUTES,), 1, LEN + 1, dtype=jnp.int32)
    order = jax.random.permutation(second_key, ROUTES)
    values = values.at[order[0]].set(LEN)
    values = values.at[order[1]].set(1)
    return values.astype(jnp.int32)


def levels(rng, shape, cuts, smallest, largest):
    loudness = 1.0
    for axis_at, shards_of in cuts:
        draws = jax.random.uniform(jax.random.fold_in(jax.random.fold_in(rng, 6), axis_at), (shards_of,), jnp.float32, smallest / len(cuts), largest / len(cuts))
        loudness = loudness * jnp.repeat(jnp.exp(draws), shape[axis_at] // shards_of).reshape((-1,) + (1,) * (len(shape) - 1 - axis_at))
    return loudness


def gaussian(key, extent, width, limit, pieces=(), kind=jnp.bfloat16):
    array = jax.random.normal(key, extent, jnp.float32) * width
    if len(pieces) > 0:
        array = levels(key, extent, pieces, -0.22, 0.18) * array
    return jnp.clip(array, min=-limit, max=limit).astype(kind)


def setup_inputs(seed: int = 0) -> dict:
    splits = jax.random.split(jax.random.key(seed), 10)
    inputs = gaussian(splits[0], (TOKENS, D), 1.0, 6.0, ((0, 32),))
    cotangent = gaussian(splits[1], (TOKENS, D), 1.0, 6.0, ((0, 32),))
    gate_pre = gaussian(splits[2], (TOKENS, FF), 1.5, 8.0, ((0, 8), (1, 4)))
    up_pre = gaussian(splits[3], (TOKENS, FF), 1.0, 6.0, ((0, 8), (1, 4)))
    w_down = gaussian(splits[4], (FF, D), FF ** -0.5, 0.046875, ((0, 4), (1, 8)))
    proj_model = gaussian(splits[5], (D, 2 * RANK), D ** -0.5, 0.09375)
    proj_hidden = gaussian(splits[6], (FF, 2 * RANK), FF ** -0.5, 0.046875, ((0, 4),))
    queries = gaussian(splits[7], (QUERIES, FEATURES), (RANK * RANK // 2) ** -0.5, 0.125, ((0, 4), (1, 8)))
    lengths = draw_lengths(jax.random.fold_in(splits[9], 71), 0)
    return dict(inputs=inputs, cotangent=cotangent, gate_pre=gate_pre, up_pre=up_pre, w_down=w_down, proj_model=proj_model, proj_hidden=proj_hidden, queries=queries, lengths=lengths)


def reference(inputs, cotangent, gate_pre, up_pre, w_down, proj_model, proj_hidden, queries, lengths):
    scale = 1.0 / math.sqrt(LEN)

    def one_route(item):
        x_rows, g_rows, gate_rows, up_rows, length = item
        act = jax.nn.silu(gate_rows.astype(jnp.float32))
        hidden = (act * up_rows.astype(jnp.float32)).astype(jnp.bfloat16)
        hidden_grad = jnp.dot(g_rows, w_down.T, preferred_element_type=jnp.float32)
        up_grad = (hidden_grad * act).astype(jnp.bfloat16)
        in_fac = jnp.dot(x_rows, proj_model[:, :RANK], preferred_element_type=jnp.float32)
        out_fac = jnp.dot(g_rows, proj_model[:, RANK:], preferred_element_type=jnp.float32)
        up_fac = jnp.dot(up_grad, proj_hidden[:, :RANK], preferred_element_type=jnp.float32)
        hid_fac = jnp.dot(hidden, proj_hidden[:, RANK:], preferred_element_type=jnp.float32)
        keep = (jnp.arange(LEN, dtype=jnp.int32) < length).astype(jnp.float32) * scale
        grad_up = jnp.dot((in_fac * keep[:, None]).T, up_fac, precision=lax.Precision.HIGHEST)
        grad_down = jnp.dot((hid_fac * keep[:, None]).T, out_fac, precision=lax.Precision.HIGHEST)
        return jnp.concatenate([grad_up.reshape(-1), grad_down.reshape(-1)])
    items = (inputs.reshape(ROUTES, LEN, D), cotangent.reshape(ROUTES, LEN, D), gate_pre.reshape(ROUTES, LEN, FF), up_pre.reshape(ROUTES, LEN, FF), lengths)
    features = lax.map(one_route, items)
    return jnp.dot(features, queries.astype(jnp.float32).T, precision=lax.Precision.HIGHEST)
```

```python
import functools
import math

import jax
import jax.numpy as jnp
from jax import lax
from jax.experimental import pallas as pl
from jax.experimental.pallas import tpu as pltpu
from jax.sharding import PartitionSpec as P

MESH = pl.DeviceIdType.MESH
WINDOW = 4
AHEAD = 2


def both(*terms):
    out = terms[0]
    for term in terms[1:]:
        out = jnp.logical_and(out, term)
    return out


def silu(v):
    return v / (1.0 + jnp.exp(-v))


def kernel(
    N, T, K, F, START,
    x_ref, cot_ref, gate_ref, up_ref, w_ref, pm_ref, ph_ref, q_ref,
    up_out, hid_out, in_out, outf_out, q_all,
    w_all, cot_all, ext_cot, gate_v, up_v, ext_gate, ext_acc, ret, x_v, pm_v, ph_v,
    bulk, up_sem, w_snd, w_rcv, q_snd, q_rcv, c_snd, c_rcv, f_snd, f_rcv, e_snd, e_rcv, g_snd, g_rcv, r_sem,
):
    dp = lax.axis_index("dp")
    t = lax.axis_index("tensor")
    z = dp // 2
    c = dp % 2
    R, cols = w_all.shape[1], w_ref.shape[2]
    mb = cot_ref.shape[0]
    qc = q_ref.shape[1]
    E = K - F
    above, below, sib = (dp + 2, t), (dp - 2, t), (dp + 1 - 2 * c, t)
    peers = [(dp, (t + d) % T) for d in range(1, T)]
    low_end, high_end = z == 0, z == N - 1
    at_end = jnp.logical_or(low_end, high_end)
    host = jnp.logical_or(z == 1, z == N - 2)

    rows = pl.ds(pl.multiple_of(t * mb, mb), mb)

    def w_cols(plane, core):
        return pl.ds(pl.multiple_of((2 * plane + core) * cols, cols), cols)

    def q_cols(plane, core):
        return pl.ds(pl.multiple_of((2 * plane + core) * qc, qc), qc)

    loads = [
        pltpu.make_async_copy(x_ref, x_v, bulk.at[0]),
        pltpu.make_async_copy(pm_ref, pm_v, bulk.at[1]),
        pltpu.make_async_copy(gate_ref, gate_v, bulk.at[2]),
        pltpu.make_async_copy(ph_ref, ph_v, bulk.at[3]),
        pltpu.make_async_copy(cot_ref, cot_all.at[rows], bulk.at[4]),
        pltpu.make_async_copy(q_ref, q_all.at[:, q_cols(z, c)], bulk.at[5]),
        pltpu.make_async_copy(w_ref, w_all.at[:, :, w_cols(z, c)], bulk.at[6]),
    ]
    for load in loads:
        load.start()

    barrier = pltpu.get_barrier_semaphore()
    for peer in [sib] + peers:
        pl.semaphore_signal(barrier, inc=1, device_id=peer, device_id_type=MESH)
    for cond, peer in ((z < N - 1, above), (z > 0, below)):

        @pl.when(cond)
        def _():
            pl.semaphore_signal(barrier, inc=1, device_id=peer, device_id_type=MESH)

    pl.semaphore_wait(barrier, T + 2 - (z + 1) // N - (N - z) // N)

    def remote(src, dst, ssem, rsem, peer):
        return pltpu.make_async_remote_copy(
            src_ref=src, dst_ref=dst, send_sem=ssem, recv_sem=rsem, device_id=peer, device_id_type=MESH
        )

    ends = ((low_end, above), (high_end, below))
    e_out = [remote(cot_ref, ext_cot.at[rows], e_snd.at[0], e_rcv.at[0], peer) for _, peer in ends]
    if E:
        for (cond, _), copy in zip(ends, e_out):
            pl.when(cond)(copy.start)

    def mine(k):
        return jnp.logical_or(jnp.logical_not(at_end), k < F)

    def go_up(k):
        return jnp.logical_and(z < N - 1, jnp.logical_or(z + 1 < N - 1, k < F))

    def go_down(k):
        return jnp.logical_and(z > 0, jnp.logical_or(z - 1 > 0, k < F))

    def w_push(index, src_of, plane, cond_of, peer, k, start=True):
        def copy(j):
            return remote(
                src_of(j),
                w_all.at[j, :, w_cols(plane, c)],
                w_snd.at[index, j % WINDOW],
                w_rcv.at[2 * plane + c, j],
                peer,
            )

        @pl.when(both(k >= WINDOW, k < K + WINDOW, cond_of(k - WINDOW)))
        def _():
            copy(k - WINDOW).wait_send()

        if start:

            @pl.when(both(k < K, cond_of(k)))
            def _():
                copy(k).start()

    def own(k, start=True):
        src = lambda j: w_ref.at[j]
        w_push(0, src, z, go_up, above, k, start)
        w_push(N, src, z, go_down, below, k, start)
        w_push(2 * N, src, z, mine, sib, k, start)

    def relay(k, start=True):
        for d in range(1, N):
            for upward in (True, False):
                plane = z - d if upward else z + d
                valid = plane >= 0 if upward else plane <= N - 1
                got = lambda j, valid=valid: jnp.logical_and(valid, mine(j))
                go = go_up if upward else go_down
                onward = lambda j, valid=valid, go=go: jnp.logical_and(valid, go(j))
                src = lambda j, plane=plane: w_all.at[j, :, w_cols(plane, c)]
                if start:

                    @pl.when(got(k))
                    def _():
                        remote(
                            src(k), src(k), w_snd.at[0, 0], w_rcv.at[2 * plane + c, k], sib
                        ).wait_recv()

                base = 0 if upward else N
                w_push(base + d, src, plane, onward, above if upward else below, k, start)
                w_push(2 * N + base + d, src, plane, got, sib, k, start)

    def q_copy(index, src, plane, peer):
        return remote(
            src, q_all.at[:, q_cols(plane, c)], q_snd.at[index], q_rcv.at[2 * plane + c], peer
        )

    def q_own(method):
        for index, cond, peer in ((0, z < N - 1, above), (N, z > 0, below), (2 * N, None, sib)):
            copy = q_copy(index, q_ref, z, peer)
            act = copy.start if method == "start" else copy.wait_send
            act() if cond is None else pl.when(cond)(act)

    def q_relay(method):
        for d in range(1, N):
            for upward in (True, False):
                plane = z - d if upward else z + d
                valid = plane >= 0 if upward else plane <= N - 1
                base = 0 if upward else N
                src = q_all.at[:, q_cols(plane, c)]
                far = z < N - 1 if upward else z > 0
                onward = q_copy(base + d, src, plane, above if upward else below)
                over = q_copy(2 * N + base + d, src, plane, sib)

                @pl.when(valid)
                def _():
                    if method == "start":
                        over.wait_recv()
                        over.start()
                        pl.when(far)(onward.start)
                    else:
                        over.wait_send()
                        pl.when(far)(onward.wait_send)

    for k in range(min(AHEAD, K)):
        own(jnp.int32(k))

    c_out = [
        remote(cot_ref, cot_all.at[rows], c_snd.at[d], c_rcv.at[d], peer) for d, peer in enumerate(peers)
    ]
    for copy in c_out:
        copy.start()
    q_own("start")

    loads[0].wait()
    loads[1].wait()
    in_out[rows, :] = jnp.dot(x_v[...], pm_v[...], preferred_element_type=jnp.float32)
    f_out = [
        remote(in_out.at[rows], in_out.at[rows], f_snd.at[d], f_rcv.at[d], peer)
        for d, peer in enumerate(peers)
    ]
    for copy in f_out:
        copy.start()
    for load in loads[2:]:
        load.wait()

    up_out[...] = jnp.zeros_like(up_out)
    hid_out[...] = jnp.zeros_like(hid_out)
    ext_acc[...] = jnp.zeros_like(ext_acc)

    def lanes(k):
        return pl.ds(pl.multiple_of(k * R, R), R)

    def up_load(k):
        return pltpu.make_async_copy(up_ref.at[:, lanes(k)], up_v.at[k % 2], up_sem.at[k % 2])

    up_load(jnp.int32(0)).start()

    def hid(k):
        @pl.when(k + 1 < K)
        def _():
            up_load(k + 1).start()

        up_load(k).wait()
        act = silu(gate_v[:, lanes(k)].astype(jnp.float32))
        hidden = (act * up_v[k % 2].astype(jnp.float32)).astype(jnp.bfloat16)
        hid_out[...] += jnp.dot(hidden, ph_v[k], preferred_element_type=jnp.float32)

    def product(cot, act, k, total):
        grad = lax.dot_general(
            cot[...], w_all[k], (((1,), (1,)), ((), ())), preferred_element_type=jnp.float32
        )
        up_grad = (grad * act).astype(jnp.bfloat16)
        total[...] += jnp.dot(up_grad, ph_v[k], preferred_element_type=jnp.float32)

    def main(k):
        @pl.when(mine(k))
        def _():
            for plane in range(N):
                ref = w_all.at[k, :, w_cols(plane, 1 - c)]
                remote(ref, ref, w_snd.at[0, 0], w_rcv.at[2 * plane + 1 - c, k], sib).wait_recv()
            product(cot_all, silu(gate_v[:, lanes(k)].astype(jnp.float32)), k, up_out)

    def ext(j):
        ref = ext_gate.at[j]
        remote(ref, ref, g_snd.at[j], g_rcv.at[j], sib).wait_recv()
        product(ext_cot, silu(ref[...].astype(jnp.float32)), F + j, ext_acc)

    e_on = [
        remote(ext_cot.at[rows], ext_cot.at[rows], e_snd.at[d], e_rcv.at[d], peer)
        for d, peer in enumerate(peers, 1)
    ]

    def g_copy(j, peer):
        return remote(gate_ref.at[:, lanes(F + j)], ext_gate.at[j], g_snd.at[j], g_rcv.at[j], peer)

    def step(s, carry):
        own(s + AHEAD)
        if E:
            for cond, peer in ends:

                @pl.when(both(cond, s % 2 == 0, s // 2 < E))
                def _():
                    g_copy(s // 2, peer).start()

            @pl.when(both(host, s == 2))
            def _():
                e_out[0].wait_recv()
                for copy in e_on:
                    copy.start()

        relay(s)

        @pl.when(s == 1)
        def _():
            q_relay("start")

        hid(s)

        @pl.when(s == START)
        def _():
            for copy in c_out:
                copy.wait_recv()
            outf_out[...] = jnp.dot(cot_all[...], pm_v[...], preferred_element_type=jnp.float32)

        def catch_up(i, carry):
            k = 2 * (s - START) + i

            @pl.when(both(k >= 0, k < s))
            def _():
                main(k)

            return carry

        lax.fori_loop(0, 2, catch_up, 0)
        return carry

    lax.fori_loop(0, K, step, 0)

    def rest(k, carry):
        main(k)
        return carry

    lax.fori_loop(min(2 * (K - START), K - 1), K, rest, 0)

    if E:

        @pl.when(host)
        def _():
            for copy in e_on:
                copy.wait_recv()
            lax.fori_loop(0, E, lambda j, carry: (ext(j), carry)[1], 0)

        r_out = [remote(ext_acc, ret, r_sem.at[0], r_sem.at[1], peer) for peer in (below, above)]
        for cond, copy in zip((z == 1, z == N - 2), r_out):
            pl.when(cond)(copy.start)

        @pl.when(at_end)
        def _():
            r_out[0].wait_recv()
            up_out[...] += ret[...]

        for cond, copy in zip((z == 1, z == N - 2), r_out):
            pl.when(cond)(copy.wait_send)

        @pl.when(host)
        def _():
            for copy in e_on:
                copy.wait_send()

        for (cond, peer), copy in zip(ends, e_out):

            @pl.when(cond)
            def _():
                copy.wait_send()
                for j in range(E):
                    g_copy(j, peer).wait_send()

    for copy in f_out + c_out:
        copy.wait_send()
    for copy in f_out:
        copy.wait_recv()
    for plane in range(N):
        ref = q_all.at[:, q_cols(plane, 1 - c)]
        remote(ref, ref, q_snd.at[0], q_rcv.at[2 * plane + 1 - c], sib).wait_recv()
    q_own("wait")
    q_relay("wait")

    def drain_own(k, carry):
        own(k, False)
        return carry

    def drain_relay(k, carry):
        relay(k, False)
        return carry

    lax.fori_loop(K + AHEAD, K + WINDOW, drain_own, 0)
    lax.fori_loop(K, K + WINDOW, drain_relay, 0)


def gather_and_project(N, T, x, cot, gate, up, w, pm, ph, q):
    tokens, hidden = gate.shape
    R = 256 if hidden % 256 == 0 else 128
    K = hidden // R
    F = K if N < 4 else -(-9 * K // 14)
    E = max(K - F, 1)
    D = cot.shape[1]
    width = pm.shape[1]
    start = K // 2
    f32, bf16 = jnp.float32, jnp.bfloat16
    dma = pltpu.SemaphoreType.DMA
    vmem = pl.BlockSpec(memory_space=pltpu.VMEM)
    return pl.pallas_call(
        functools.partial(kernel, N, T, K, F, start),
        out_shape=[jax.ShapeDtypeStruct((tokens, width), f32)] * 4
        + [jax.ShapeDtypeStruct((q.shape[0], 2 * N * q.shape[1]), bf16)],
        in_specs=[pl.BlockSpec(memory_space=pl.ANY)] * 8,
        out_specs=[vmem] * 5,
        scratch_shapes=[
            pltpu.VMEM((K, R, D), bf16),
            pltpu.VMEM((tokens, D), bf16),
            pltpu.VMEM((tokens, D), bf16),
            pltpu.VMEM((tokens, hidden), bf16),
            pltpu.VMEM((2, tokens, R), bf16),
            pltpu.VMEM((E, tokens, R), bf16),
            pltpu.VMEM((tokens, width), f32),
            pltpu.VMEM((tokens, width), f32),
            pltpu.VMEM(x.shape, bf16),
            pltpu.VMEM(pm.shape, bf16),
            pltpu.VMEM((K, R, width), bf16),
            dma((7,)),
            dma((2,)),
            dma((4 * N, WINDOW)),
            dma((2 * N, K)),
            dma((4 * N,)),
            dma((2 * N,)),
            dma((T,)),
            dma((T,)),
            dma((T,)),
            dma((T,)),
            dma((T,)),
            dma((T,)),
            dma((E,)),
            dma((E,)),
            dma((2,)),
        ],
        compiler_params=pltpu.CompilerParams(
            collective_id=0, has_side_effects=True, vmem_limit_bytes=61 * 1024 * 1024
        ),
    )(x, cot, gate, up, w.reshape(K, R, w.shape[1]), pm, ph.reshape(K, R, width), q)


def route_features(keep, left, right):
    routes, count = keep.shape
    rank = left.shape[1]
    left = (left.reshape(routes, count, rank) * keep[:, :, None])
    right = right.reshape(routes, count, rank)
    return jnp.einsum("eti,etj->eij", left, right, precision=lax.Precision.HIGHEST).reshape(
        routes, rank * rank
    )


def per_device(
    N, T, inputs, cotangent, gate_pre, up_pre, w_down, proj_model, proj_hidden, queries, lengths
):
    rank = proj_model.shape[1] // 2
    routes = lengths.shape[0]
    route_len = gate_pre.shape[0] // routes
    up_part, hid_part, in_fac, out_fac, query_rows = gather_and_project(
        N, T, inputs, cotangent, gate_pre, up_pre, w_down, proj_model, proj_hidden, queries
    )
    scale = 1.0 / math.sqrt(route_len)
    position = jnp.arange(route_len, dtype=jnp.int32)
    keep = (position[None, :] < lengths[:, None]).astype(jnp.float32) * scale
    part = jnp.concatenate(
        [
            route_features(keep, in_fac[:, :rank], up_part[:, :rank]),
            route_features(keep, hid_part[:, rank:], out_fac[:, rank:]),
        ],
        axis=1,
    )
    features = lax.psum(part, "tensor")
    return jnp.dot(features, query_rows.astype(jnp.float32).T, precision=lax.Precision.HIGHEST)


def solution(mesh):
    return jax.shard_map(
        functools.partial(per_device, mesh.shape["dp"] // 2, mesh.shape["tensor"]),
        mesh=mesh,
        in_specs=(
            P(("dp", "tensor"), None),
            P(("dp", "tensor"), None),
            P("dp", "tensor"),
            P("dp", "tensor"),
            P("tensor", "dp"),
            P(),
            P("tensor", None),
            P("tensor", "dp"),
            P("dp"),
        ),
        out_specs=P("dp", "tensor"),
        check_vma=False,
    )
```

```python
import functools
import math

import jax
import jax.numpy as jnp
from jax import lax
from jax.experimental import pallas as pl
from jax.experimental.pallas import tpu as pltpu
from jax.sharding import PartitionSpec as P

MESH = pl.DeviceIdType.MESH
WINDOW = 14
AHEAD = 4
EARLY = 5


def both(*terms):
    out = terms[0]
    for term in terms[1:]:
        out = jnp.logical_and(out, term)
    return out


def silu(v):
    return v / (1.0 + jnp.exp(-v))


def kernel(
    N, T, K, F, START,
    x_ref, cot_ref, gate_ref, up_ref, w_ref, pm_ref, ph_ref, q_ref, len_ref,
    feat_out, q_all,
    up_out, hid_out, in_out, outf_out, part, parts, w_all, cot_all, ext_cot, gate_v, up_v, ext_gate, ext_acc, ret, x_v, pm_v, ph_v,
    bulk, up_sem, w_snd, w_rcv, q_snd, q_rcv, c_snd, c_rcv, f_snd, f_rcv, e_snd, e_rcv, g_snd, g_rcv, r_sem, p_snd, p_rcv,
):
    dp = lax.axis_index("dp")
    t = lax.axis_index("tensor")
    z = dp // 2
    c = dp % 2
    R, cols = w_all.shape[1], w_ref.shape[2]
    mb = cot_ref.shape[0]
    qc = q_ref.shape[1]
    E = K - F
    above, below, sib = (dp + 2, t), (dp - 2, t), (dp + 1 - 2 * c, t)
    peers = [(dp, (t + d) % T) for d in range(1, T)]
    low_end, high_end = z == 0, z == N - 1
    at_end = jnp.logical_or(low_end, high_end)
    host = jnp.logical_or(z == 1, z == N - 2)
    EVEN = 2 * START - N + 1

    rows = pl.ds(pl.multiple_of(t * mb, mb), mb)

    def w_cols(plane, core):
        return pl.ds(pl.multiple_of((2 * plane + core) * cols, cols), cols)

    def q_cols(plane, core):
        return pl.ds(pl.multiple_of((2 * plane + core) * qc, qc), qc)

    loads = [
        pltpu.make_async_copy(x_ref, x_v, bulk.at[0]),
        pltpu.make_async_copy(pm_ref, pm_v, bulk.at[1]),
        pltpu.make_async_copy(gate_ref, gate_v, bulk.at[2]),
        pltpu.make_async_copy(ph_ref, ph_v, bulk.at[3]),
        pltpu.make_async_copy(cot_ref, cot_all.at[rows], bulk.at[4]),
        pltpu.make_async_copy(q_ref, q_all.at[:, q_cols(z, c)], bulk.at[5]),
        pltpu.make_async_copy(w_ref, w_all.at[:, :, w_cols(z, c)], bulk.at[6]),
    ]
    for load in loads:
        load.start()

    barrier = pltpu.get_barrier_semaphore()
    for peer in [sib] + peers:
        pl.semaphore_signal(barrier, inc=1, device_id=peer, device_id_type=MESH)
    for cond, peer in ((z < N - 1, above), (z > 0, below)):

        @pl.when(cond)
        def _():
            pl.semaphore_signal(barrier, inc=1, device_id=peer, device_id_type=MESH)

    pl.semaphore_wait(barrier, T + 2 - (z + 1) // N - (N - z) // N)

    def remote(src, dst, ssem, rsem, peer):
        return pltpu.make_async_remote_copy(
            src_ref=src, dst_ref=dst, send_sem=ssem, recv_sem=rsem, device_id=peer, device_id_type=MESH
        )

    ends = ((low_end, above), (high_end, below))
    e_out = [remote(cot_ref, ext_cot.at[rows], e_snd.at[0], e_rcv.at[0], peer) for _, peer in ends]
    if E:
        for (cond, _), copy in zip(ends, e_out):
            pl.when(cond)(copy.start)

    def mine(k):
        return jnp.logical_or(jnp.logical_not(at_end), k < F)

    def go_up(k):
        return jnp.logical_and(z < N - 1, jnp.logical_or(z + 1 < N - 1, k < F))

    def go_down(k):
        return jnp.logical_and(z > 0, jnp.logical_or(z - 1 > 0, k < F))

    def w_push(index, src_of, plane, cond_of, peer, k, start=True):
        def copy(j):
            return remote(
                src_of(j),
                w_all.at[j, :, w_cols(plane, c)],
                w_snd.at[index, j % WINDOW],
                w_rcv.at[2 * plane + c, j],
                peer,
            )

        most = K if start else K + WINDOW

        @pl.when(both(k >= WINDOW, k < most, cond_of(k - WINDOW)))
        def _():
            copy(k - WINDOW).wait_send()

        if start:

            @pl.when(both(k >= 0, k < K, cond_of(k)))
            def _():
                copy(k).start()

    def own(k, start=True):
        src = lambda j: w_ref.at[j]
        w_push(0, src, z, go_up, above, k, start)
        w_push(N, src, z, go_down, below, k, start)
        w_push(2 * N, src, z, mine, sib, k, start)

    def relay(first, start=True):
        for d in range(1, N):
            k = first - d + 1 if start else first
            for upward in (True, False):
                plane = z - d if upward else z + d
                valid = plane >= 0 if upward else plane <= N - 1
                got = lambda j, valid=valid: jnp.logical_and(valid, mine(j))
                go = go_up if upward else go_down
                onward = lambda j, valid=valid, go=go: jnp.logical_and(valid, go(j))
                src = lambda j, plane=plane: w_all.at[j, :, w_cols(plane, c)]
                if start:

                    @pl.when(both(k >= 0, k < K, got(k)))
                    def _():
                        remote(
                            src(k), src(k), w_snd.at[0, 0], w_rcv.at[2 * plane + c, k], sib
                        ).wait_recv()

                base = 0 if upward else N
                w_push(base + d, src, plane, onward, above if upward else below, k, start)
                w_push(2 * N + base + d, src, plane, got, sib, k, start)

    def q_copy(index, src, plane, peer):
        return remote(
            src, q_all.at[:, q_cols(plane, c)], q_snd.at[index], q_rcv.at[2 * plane + c], peer
        )

    def q_own(method):
        for index, cond, peer in ((0, z < N - 1, above), (N, z > 0, below), (2 * N, None, sib)):
            copy = q_copy(index, q_ref, z, peer)
            act = copy.start if method == "start" else copy.wait_send
            act() if cond is None else pl.when(cond)(act)

    def q_relay(method, distances):
        for d in distances:
            for upward in (True, False):
                plane = z - d if upward else z + d
                valid = plane >= 0 if upward else plane <= N - 1
                base = 0 if upward else N
                src = q_all.at[:, q_cols(plane, c)]
                far = z < N - 1 if upward else z > 0
                onward = q_copy(base + d, src, plane, above if upward else below)
                over = q_copy(2 * N + base + d, src, plane, sib)

                @pl.when(valid)
                def _():
                    if method == "start":
                        over.wait_recv()
                        over.start()
                        pl.when(far)(onward.start)
                    else:
                        over.wait_send()
                        pl.when(far)(onward.wait_send)

    for k in range(min(AHEAD, K)):
        own(jnp.int32(k))

    c_out = [
        remote(cot_ref, cot_all.at[rows], c_snd.at[d], c_rcv.at[d], peer) for d, peer in enumerate(peers)
    ]
    for copy in c_out:
        copy.start()
    q_own("start")

    loads[0].wait()
    loads[1].wait()
    in_out[rows, :] = jnp.dot(x_v[...], pm_v[...], preferred_element_type=jnp.float32)
    f_out = [
        remote(in_out.at[rows], in_out.at[rows], f_snd.at[d], f_rcv.at[d], peer)
        for d, peer in enumerate(peers)
    ]
    for copy in f_out:
        copy.start()
    for load in loads[2:]:
        load.wait()

    up_out[...] = jnp.zeros_like(up_out)
    hid_out[...] = jnp.zeros_like(hid_out)
    ext_acc[...] = jnp.zeros_like(ext_acc)

    def lanes(k):
        return pl.ds(pl.multiple_of(k * R, R), R)

    def up_load(k):
        return pltpu.make_async_copy(up_ref.at[:, lanes(k)], up_v.at[k % 2], up_sem.at[k % 2])

    up_load(jnp.int32(0)).start()

    def hid(k):
        @pl.when(k + 1 < K)
        def _():
            up_load(k + 1).start()

        up_load(k).wait()
        act = silu(gate_v[:, lanes(k)].astype(jnp.float32))
        hidden = (act * up_v[k % 2].astype(jnp.float32)).astype(jnp.bfloat16)
        hid_out[...] += jnp.dot(hidden, ph_v[k], preferred_element_type=jnp.float32)

    def product(cot, act, k, total):
        grad = lax.dot_general(
            cot[...], w_all[k], (((1,), (1,)), ((), ())), preferred_element_type=jnp.float32
        )
        up_grad = (grad * act).astype(jnp.bfloat16)
        total[...] += jnp.dot(up_grad, ph_v[k], preferred_element_type=jnp.float32)

    def main(k):
        @pl.when(mine(k))
        def _():
            for plane in range(N):
                ref = w_all.at[k, :, w_cols(plane, 1 - c)]
                remote(ref, ref, w_snd.at[0, 0], w_rcv.at[2 * plane + 1 - c, k], sib).wait_recv()
            product(cot_all, silu(gate_v[:, lanes(k)].astype(jnp.float32)), k, up_out)

    def ext(j):
        ref = ext_gate.at[j]
        remote(ref, ref, g_snd.at[j], g_rcv.at[j], sib).wait_recv()
        product(ext_cot, silu(ref[...].astype(jnp.float32)), F + j, ext_acc)

    e_on = [
        remote(ext_cot.at[rows], ext_cot.at[rows], e_snd.at[d], e_rcv.at[d], peer)
        for d, peer in enumerate(peers, 1)
    ]

    def g_copy(j, peer):
        return remote(gate_ref.at[:, lanes(F + j)], ext_gate.at[j], g_snd.at[j], g_rcv.at[j], peer)

    def step(s, carry):
        own(s + AHEAD)
        if E:
            for cond, peer in ends:

                @pl.when(both(cond, s % 2 == 0, s // 2 < E))
                def _():
                    g_copy(s // 2, peer).start()

            @pl.when(both(host, s == EARLY))
            def _():
                e_out[0].wait_recv()
                for copy in e_on:
                    copy.start()

        relay(s)

        for d in range(1, N):

            @pl.when(s == d + 2)
            def _():
                q_relay("start", [d])

        pl.when(s < K)(functools.partial(hid, s))

        @pl.when(s == START)
        def _():
            for copy in c_out:
                copy.wait_recv()
            outf_out[...] = jnp.dot(cot_all[...], pm_v[...], preferred_element_type=jnp.float32)

        def catch_up(i, carry):
            k = 2 * (s - START) + i
            pl.when(k < K)(functools.partial(main, k))
            return carry

        @pl.when(both(s >= START, s < EVEN))
        def _():
            lax.fori_loop(0, 2, catch_up, 0)

        pl.when(both(s >= EVEN, s - N + 1 < K))(lambda: main(s - N + 1))
        return carry

    lax.fori_loop(0, K + N - 2, step, 0)

    if E:

        @pl.when(host)
        def _():
            for copy in e_on:
                copy.wait_recv()
            lax.fori_loop(0, E - 1, lambda j, carry: (ext(j), carry)[1], 0)

    main(K - 1)

    if E:
        pl.when(host)(lambda: ext(E - 1))
        r_out = [remote(ext_acc, ret, r_sem.at[0], r_sem.at[1], peer) for peer in (below, above)]
        for cond, copy in zip((z == 1, z == N - 2), r_out):
            pl.when(cond)(copy.start)

        @pl.when(at_end)
        def _():
            r_out[0].wait_recv()
            up_out[...] += ret[...]

    for copy in f_out:
        copy.wait_recv()
    routes = len_ref.shape[0]
    span = up_out.shape[0] // routes
    rank = up_out.shape[1] // 2
    position = lax.broadcasted_iota(jnp.int32, (span, 2 * rank), 0)
    lane = lax.broadcasted_iota(jnp.int32, (rank, 2 * rank), 1)

    def outer(left, right):
        return lax.dot_general(
            left,
            right,
            (((0,), (0,)), ((), ())),
            precision=lax.Precision.HIGHEST,
            preferred_element_type=jnp.float32,
        )

    for e in range(routes):
        at = pl.ds(e * span, span)
        keep = jnp.where(position < len_ref[e], 1.0 / math.sqrt(span), 0.0).astype(jnp.float32)
        grad_up = outer(in_out[at, :] * keep, up_out[at, :])
        grad_down = outer(hid_out[at, :] * keep, outf_out[at, :])
        part[pl.ds(e * rank, rank), :] = jnp.where(lane < rank, grad_up[:rank], grad_down[rank:])
    p_out = [
        remote(part, parts.at[d], p_snd.at[d], p_rcv.at[d], peer) for d, peer in enumerate(peers)
    ]
    for copy in p_out:
        copy.start()

    if E:

        for cond, copy in zip((z == 1, z == N - 2), r_out):
            pl.when(cond)(copy.wait_send)

        @pl.when(host)
        def _():
            for copy in e_on:
                copy.wait_send()

        for (cond, peer), copy in zip(ends, e_out):

            @pl.when(cond)
            def _():
                copy.wait_send()
                for j in range(E):
                    g_copy(j, peer).wait_send()

    for copy in f_out + c_out:
        copy.wait_send()
    for plane in range(N):
        ref = q_all.at[:, q_cols(plane, 1 - c)]
        remote(ref, ref, q_snd.at[0], q_rcv.at[2 * plane + 1 - c], sib).wait_recv()
    q_own("wait")
    q_relay("wait", range(1, N))

    def drain_own(k, carry):
        own(k, False)
        return carry

    def drain_relay(k, carry):
        relay(k, False)
        return carry

    lax.fori_loop(K, K + WINDOW, drain_own, 0)
    lax.fori_loop(K, K + WINDOW, drain_relay, 0)

    total = part[...]
    for d, copy in enumerate(p_out):
        copy.wait_recv()
        total = total + parts[d]
    feat_out[...] = total
    for copy in p_out:
        copy.wait_send()


def gather_and_project(N, T, x, cot, gate, up, w, pm, ph, q, lengths):
    tokens, hidden = gate.shape
    R = 256 if hidden % 256 == 0 else 128
    K = hidden // R
    F = K if N < 4 else -(-9 * K // 14)
    E = max(K - F, 1)
    D = cot.shape[1]
    width = pm.shape[1]
    start = max(K // 2 + 1, N)
    f32, bf16 = jnp.float32, jnp.bfloat16
    dma = pltpu.SemaphoreType.DMA
    vmem = pl.BlockSpec(memory_space=pltpu.VMEM)
    return pl.pallas_call(
        functools.partial(kernel, N, T, K, F, start),
        out_shape=[
            jax.ShapeDtypeStruct((lengths.shape[0] * width // 2, width), f32),
            jax.ShapeDtypeStruct((q.shape[0], 2 * N * q.shape[1]), bf16),
        ],
        in_specs=[pl.BlockSpec(memory_space=pl.ANY)] * 8
        + [pl.BlockSpec(memory_space=pltpu.SMEM)],
        out_specs=[vmem] * 2,
        scratch_shapes=[
            pltpu.VMEM((tokens, width), f32),
            pltpu.VMEM((tokens, width), f32),
            pltpu.VMEM((tokens, width), f32),
            pltpu.VMEM((tokens, width), f32),
            pltpu.VMEM((lengths.shape[0] * width // 2, width), f32),
            pltpu.VMEM((T, lengths.shape[0] * width // 2, width), f32),
            pltpu.VMEM((K, R, D), bf16),
            pltpu.VMEM((tokens, D), bf16),
            pltpu.VMEM((tokens, D), bf16),
            pltpu.VMEM((tokens, hidden), bf16),
            pltpu.VMEM((2, tokens, R), bf16),
            pltpu.VMEM((E, tokens, R), bf16),
            pltpu.VMEM((tokens, width), f32),
            pltpu.VMEM((tokens, width), f32),
            pltpu.VMEM(x.shape, bf16),
            pltpu.VMEM(pm.shape, bf16),
            pltpu.VMEM((K, R, width), bf16),
            dma((7,)),
            dma((2,)),
            dma((4 * N, WINDOW)),
            dma((2 * N, K)),
            dma((4 * N,)),
            dma((2 * N,)),
            dma((T,)),
            dma((T,)),
            dma((T,)),
            dma((T,)),
            dma((T,)),
            dma((T,)),
            dma((E,)),
            dma((E,)),
            dma((2,)),
            dma((T,)),
            dma((T,)),
        ],
        compiler_params=pltpu.CompilerParams(
            collective_id=0, has_side_effects=True, vmem_limit_bytes=61 * 1024 * 1024
        ),
    )(x, cot, gate, up, w.reshape(K, R, w.shape[1]), pm, ph.reshape(K, R, width), q, lengths)


def per_device(
    N, T, inputs, cotangent, gate_pre, up_pre, w_down, proj_model, proj_hidden, queries, lengths
):
    rank = proj_model.shape[1] // 2
    routes = lengths.shape[0]
    features, query_rows = gather_and_project(
        N, T, inputs, cotangent, gate_pre, up_pre, w_down, proj_model, proj_hidden, queries, lengths
    )
    features = features.reshape(routes, rank, 2, rank).transpose(0, 2, 1, 3).reshape(routes, -1)
    return jnp.dot(features, query_rows.astype(jnp.float32).T, precision=lax.Precision.HIGHEST)


def solution(mesh):
    return jax.shard_map(
        functools.partial(per_device, mesh.shape["dp"] // 2, mesh.shape["tensor"]),
        mesh=mesh,
        in_specs=(
            P(("dp", "tensor"), None),
            P(("dp", "tensor"), None),
            P("dp", "tensor"),
            P("dp", "tensor"),
            P("tensor", "dp"),
            P(),
            P("tensor", None),
            P("tensor", "dp"),
            P("dp"),
        ),
        out_specs=P("dp", "tensor"),
        check_vma=False,
    )
```

```python
import functools
import math

import jax
import jax.numpy as jnp
from jax import lax
from jax.experimental import pallas as pl
from jax.experimental.pallas import tpu as pltpu
from jax.sharding import PartitionSpec as P

MESH = pl.DeviceIdType.MESH
WINDOW = 14
AHEAD = 6
EARLY = 5


def both(*terms):
    out = terms[0]
    for term in terms[1:]:
        out = jnp.logical_and(out, term)
    return out


def silu(v):
    return v / (1.0 + jnp.exp(-v))


def kernel(
    N, T, K, F, START,
    x_ref, cot_ref, gate_ref, up_ref, w_ref, pm_ref, ph_ref, q_ref, len_ref,
    feat_out, q_all,
    up_out, hid_out, in_out, outf_out, part, parts, w_all, cot_all, ext_cot, gate_v, up_v, ext_gate, ext_acc, ret, x_v, pm_v, ph_v,
    bulk, up_sem, w_snd, w_rcv, q_snd, q_rcv, c_snd, c_rcv, f_snd, f_rcv, e_snd, e_rcv, g_snd, g_rcv, r_sem, p_snd, p_rcv,
):
    dp = lax.axis_index("dp")
    t = lax.axis_index("tensor")
    z = dp // 2
    c = dp % 2
    R, cols = w_all.shape[1], w_ref.shape[2]
    mb = cot_ref.shape[0]
    qc = q_ref.shape[1]
    E = K - F
    above, below, sib = (dp + 2, t), (dp - 2, t), (dp + 1 - 2 * c, t)
    peers = [(dp, (t + d) % T) for d in range(1, T)]
    low_end, high_end = z == 0, z == N - 1
    at_end = jnp.logical_or(low_end, high_end)
    host = jnp.logical_or(z == 1, z == N - 2)
    EVEN = 2 * START - N + 1

    rows = pl.ds(pl.multiple_of(t * mb, mb), mb)

    def w_cols(plane, core):
        return pl.ds(pl.multiple_of((2 * plane + core) * cols, cols), cols)

    def q_cols(plane, core):
        return pl.ds(pl.multiple_of((2 * plane + core) * qc, qc), qc)

    loads = [
        pltpu.make_async_copy(x_ref, x_v, bulk.at[0]),
        pltpu.make_async_copy(pm_ref, pm_v, bulk.at[1]),
        pltpu.make_async_copy(gate_ref, gate_v, bulk.at[2]),
        pltpu.make_async_copy(ph_ref, ph_v, bulk.at[3]),
        pltpu.make_async_copy(cot_ref, cot_all.at[rows], bulk.at[4]),
        pltpu.make_async_copy(q_ref, q_all.at[:, q_cols(z, c)], bulk.at[5]),
        pltpu.make_async_copy(w_ref, w_all.at[:, :, w_cols(z, c)], bulk.at[6]),
    ]
    for load in loads:
        load.start()

    barrier = pltpu.get_barrier_semaphore()
    for peer in [sib] + peers:
        pl.semaphore_signal(barrier, inc=1, device_id=peer, device_id_type=MESH)
    for cond, peer in ((z < N - 1, above), (z > 0, below)):

        @pl.when(cond)
        def _():
            pl.semaphore_signal(barrier, inc=1, device_id=peer, device_id_type=MESH)

    pl.semaphore_wait(barrier, T + 2 - (z + 1) // N - (N - z) // N)

    def remote(src, dst, ssem, rsem, peer):
        return pltpu.make_async_remote_copy(
            src_ref=src, dst_ref=dst, send_sem=ssem, recv_sem=rsem, device_id=peer, device_id_type=MESH
        )

    ends = ((low_end, above), (high_end, below))
    e_out = [remote(cot_ref, ext_cot.at[rows], e_snd.at[0], e_rcv.at[0], peer) for _, peer in ends]
    if E:
        for (cond, _), copy in zip(ends, e_out):
            pl.when(cond)(copy.start)

    def mine(k):
        return jnp.logical_or(jnp.logical_not(at_end), k < F)

    def go_up(k):
        return jnp.logical_and(z < N - 1, jnp.logical_or(z + 1 < N - 1, k < F))

    def go_down(k):
        return jnp.logical_and(z > 0, jnp.logical_or(z - 1 > 0, k < F))

    def w_push(index, src_of, plane, cond_of, peer, k, start=True):
        def copy(j):
            return remote(
                src_of(j),
                w_all.at[j, :, w_cols(plane, c)],
                w_snd.at[index, j % WINDOW],
                w_rcv.at[2 * plane + c, j],
                peer,
            )

        most = K if start else K + WINDOW

        @pl.when(both(k >= WINDOW, k < most, cond_of(k - WINDOW)))
        def _():
            copy(k - WINDOW).wait_send()

        if start:

            @pl.when(both(k >= 0, k < K, cond_of(k)))
            def _():
                copy(k).start()

    def own(k, start=True):
        src = lambda j: w_ref.at[j]
        w_push(0, src, z, go_up, above, k, start)
        w_push(N, src, z, go_down, below, k, start)
        w_push(2 * N, src, z, mine, sib, k, start)

    def relay(first, start=True):
        for d in range(1, N):
            k = first - d + 1 if start else first
            for upward in (True, False):
                plane = z - d if upward else z + d
                valid = plane >= 0 if upward else plane <= N - 1
                got = lambda j, valid=valid: jnp.logical_and(valid, mine(j))
                go = go_up if upward else go_down
                onward = lambda j, valid=valid, go=go: jnp.logical_and(valid, go(j))
                src = lambda j, plane=plane: w_all.at[j, :, w_cols(plane, c)]
                if start:

                    @pl.when(both(k >= 0, k < K, got(k)))
                    def _():
                        remote(
                            src(k), src(k), w_snd.at[0, 0], w_rcv.at[2 * plane + c, k], sib
                        ).wait_recv()

                base = 0 if upward else N
                w_push(base + d, src, plane, onward, above if upward else below, k, start)
                w_push(2 * N + base + d, src, plane, got, sib, k, start)

    def q_copy(index, src, plane, peer):
        return remote(
            src, q_all.at[:, q_cols(plane, c)], q_snd.at[index], q_rcv.at[2 * plane + c], peer
        )

    def q_own(method):
        for index, cond, peer in ((0, z < N - 1, above), (N, z > 0, below), (2 * N, None, sib)):
            copy = q_copy(index, q_ref, z, peer)
            act = copy.start if method == "start" else copy.wait_send
            act() if cond is None else pl.when(cond)(act)

    def q_relay(method, distances):
        for d in distances:
            for upward in (True, False):
                plane = z - d if upward else z + d
                valid = plane >= 0 if upward else plane <= N - 1
                base = 0 if upward else N
                src = q_all.at[:, q_cols(plane, c)]
                far = z < N - 1 if upward else z > 0
                onward = q_copy(base + d, src, plane, above if upward else below)
                over = q_copy(2 * N + base + d, src, plane, sib)

                @pl.when(valid)
                def _():
                    if method == "start":
                        over.wait_recv()
                        over.start()
                        pl.when(far)(onward.start)
                    else:
                        over.wait_send()
                        pl.when(far)(onward.wait_send)

    for k in range(min(AHEAD, K)):
        own(jnp.int32(k))

    c_out = [
        remote(cot_ref, cot_all.at[rows], c_snd.at[d], c_rcv.at[d], peer) for d, peer in enumerate(peers)
    ]
    for copy in c_out:
        copy.start()
    q_own("start")

    loads[0].wait()
    loads[1].wait()
    in_out[rows, :] = jnp.dot(x_v[...], pm_v[...], preferred_element_type=jnp.float32)
    f_out = [
        remote(in_out.at[rows], in_out.at[rows], f_snd.at[d], f_rcv.at[d], peer)
        for d, peer in enumerate(peers)
    ]
    for copy in f_out:
        copy.start()
    for load in loads[2:]:
        load.wait()

    up_out[...] = jnp.zeros_like(up_out)
    hid_out[...] = jnp.zeros_like(hid_out)
    ext_acc[...] = jnp.zeros_like(ext_acc)

    def lanes(k):
        return pl.ds(pl.multiple_of(k * R, R), R)

    def up_load(k):
        return pltpu.make_async_copy(up_ref.at[:, lanes(k)], up_v.at[k % 2], up_sem.at[k % 2])

    up_load(jnp.int32(0)).start()

    def hid(k):
        @pl.when(k + 1 < K)
        def _():
            up_load(k + 1).start()

        up_load(k).wait()
        act = silu(gate_v[:, lanes(k)].astype(jnp.float32))
        hidden = (act * up_v[k % 2].astype(jnp.float32)).astype(jnp.bfloat16)
        hid_out[...] += jnp.dot(hidden, ph_v[k], preferred_element_type=jnp.float32)

    def product(cot, act, k, total):
        grad = lax.dot_general(
            cot[...], w_all[k], (((1,), (1,)), ((), ())), preferred_element_type=jnp.float32
        )
        up_grad = (grad * act).astype(jnp.bfloat16)
        total[...] += jnp.dot(up_grad, ph_v[k], preferred_element_type=jnp.float32)

    def main(k):
        @pl.when(mine(k))
        def _():
            for plane in range(N):
                ref = w_all.at[k, :, w_cols(plane, 1 - c)]
                remote(ref, ref, w_snd.at[0, 0], w_rcv.at[2 * plane + 1 - c, k], sib).wait_recv()
            product(cot_all, silu(gate_v[:, lanes(k)].astype(jnp.float32)), k, up_out)

    def ext(j):
        ref = ext_gate.at[j]
        remote(ref, ref, g_snd.at[j], g_rcv.at[j], sib).wait_recv()
        product(ext_cot, silu(ref[...].astype(jnp.float32)), F + j, ext_acc)

    e_on = [
        remote(ext_cot.at[rows], ext_cot.at[rows], e_snd.at[d], e_rcv.at[d], peer)
        for d, peer in enumerate(peers, 1)
    ]

    def g_copy(j, peer):
        return remote(gate_ref.at[:, lanes(F + j)], ext_gate.at[j], g_snd.at[j], g_rcv.at[j], peer)

    def step(s, carry):
        own(s + AHEAD)
        if E:
            for cond, peer in ends:

                @pl.when(both(cond, s % 2 == 0, s // 2 < E))
                def _():
                    g_copy(s // 2, peer).start()

            @pl.when(both(host, s == EARLY))
            def _():
                e_out[0].wait_recv()
                for copy in e_on:
                    copy.start()

        relay(s)

        for d in range(1, N):

            @pl.when(s == d + 2)
            def _():
                q_relay("start", [d])

        pl.when(s < K)(functools.partial(hid, s))

        @pl.when(s == START)
        def _():
            for copy in c_out:
                copy.wait_recv()
            outf_out[...] = jnp.dot(cot_all[...], pm_v[...], preferred_element_type=jnp.float32)

        def catch_up(i, carry):
            k = 2 * (s - START) + i
            pl.when(k < K)(functools.partial(main, k))
            return carry

        @pl.when(both(s >= START, s < EVEN))
        def _():
            lax.fori_loop(0, 2, catch_up, 0)

        pl.when(both(s >= EVEN, s - N + 1 < K))(lambda: main(s - N + 1))
        return carry

    lax.fori_loop(0, K + N - 2, step, 0)

    if E:

        @pl.when(host)
        def _():
            for copy in e_on:
                copy.wait_recv()
            lax.fori_loop(0, E - 1, lambda j, carry: (ext(j), carry)[1], 0)

    main(K - 1)

    if E:
        pl.when(host)(lambda: ext(E - 1))
        r_out = [remote(ext_acc, ret, r_sem.at[0], r_sem.at[1], peer) for peer in (below, above)]
        for cond, copy in zip((z == 1, z == N - 2), r_out):
            pl.when(cond)(copy.start)

        @pl.when(at_end)
        def _():
            r_out[0].wait_recv()
            up_out[...] += ret[...]

    for copy in f_out:
        copy.wait_recv()
    routes = len_ref.shape[0]
    span = up_out.shape[0] // routes
    rank = up_out.shape[1] // 2
    position = lax.broadcasted_iota(jnp.int32, (span, 2 * rank), 0)
    lane = lax.broadcasted_iota(jnp.int32, (rank, 2 * rank), 1)

    def outer(left, right):
        return lax.dot_general(
            left,
            right,
            (((0,), (0,)), ((), ())),
            precision=lax.Precision.HIGHEST,
            preferred_element_type=jnp.float32,
        )

    for e in range(routes):
        at = pl.ds(e * span, span)
        keep = jnp.where(position < len_ref[e], 1.0 / math.sqrt(span), 0.0).astype(jnp.float32)
        grad_up = outer(in_out[at, :] * keep, up_out[at, :])
        grad_down = outer(hid_out[at, :] * keep, outf_out[at, :])
        part[pl.ds(e * rank, rank), :] = jnp.where(lane < rank, grad_up[:rank], grad_down[rank:])
    p_out = [
        remote(part, parts.at[d], p_snd.at[d], p_rcv.at[d], peer) for d, peer in enumerate(peers)
    ]
    for copy in p_out:
        copy.start()

    if E:

        for cond, copy in zip((z == 1, z == N - 2), r_out):
            pl.when(cond)(copy.wait_send)

        @pl.when(host)
        def _():
            for copy in e_on:
                copy.wait_send()

        for (cond, peer), copy in zip(ends, e_out):

            @pl.when(cond)
            def _():
                copy.wait_send()
                for j in range(E):
                    g_copy(j, peer).wait_send()

    for copy in f_out + c_out:
        copy.wait_send()
    for plane in range(N):
        ref = q_all.at[:, q_cols(plane, 1 - c)]
        remote(ref, ref, q_snd.at[0], q_rcv.at[2 * plane + 1 - c], sib).wait_recv()
    q_own("wait")
    q_relay("wait", range(1, N))

    def drain_own(k, carry):
        own(k, False)
        return carry

    def drain_relay(k, carry):
        relay(k, False)
        return carry

    lax.fori_loop(K, K + WINDOW, drain_own, 0)
    lax.fori_loop(K, K + WINDOW, drain_relay, 0)

    total = part[...]
    for d, copy in enumerate(p_out):
        copy.wait_recv()
        total = total + parts[d]
    feat_out[...] = total
    for copy in p_out:
        copy.wait_send()


def gather_and_project(N, T, x, cot, gate, up, w, pm, ph, q, lengths):
    tokens, hidden = gate.shape
    R = 256 if hidden % 256 == 0 else 128
    K = hidden // R
    F = K if N < 4 else -(-9 * K // 14)
    E = max(K - F, 1)
    D = cot.shape[1]
    width = pm.shape[1]
    start = max(K // 2 + 1, N)
    f32, bf16 = jnp.float32, jnp.bfloat16
    dma = pltpu.SemaphoreType.DMA
    vmem = pl.BlockSpec(memory_space=pltpu.VMEM)
    return pl.pallas_call(
        functools.partial(kernel, N, T, K, F, start),
        out_shape=[
            jax.ShapeDtypeStruct((lengths.shape[0] * width // 2, width), f32),
            jax.ShapeDtypeStruct((q.shape[0], 2 * N * q.shape[1]), bf16),
        ],
        in_specs=[pl.BlockSpec(memory_space=pl.ANY)] * 8
        + [pl.BlockSpec(memory_space=pltpu.SMEM)],
        out_specs=[vmem] * 2,
        scratch_shapes=[
            pltpu.VMEM((tokens, width), f32),
            pltpu.VMEM((tokens, width), f32),
            pltpu.VMEM((tokens, width), f32),
            pltpu.VMEM((tokens, width), f32),
            pltpu.VMEM((lengths.shape[0] * width // 2, width), f32),
            pltpu.VMEM((T, lengths.shape[0] * width // 2, width), f32),
            pltpu.VMEM((K, R, D), bf16),
            pltpu.VMEM((tokens, D), bf16),
            pltpu.VMEM((tokens, D), bf16),
            pltpu.VMEM((tokens, hidden), bf16),
            pltpu.VMEM((2, tokens, R), bf16),
            pltpu.VMEM((E, tokens, R), bf16),
            pltpu.VMEM((tokens, width), f32),
            pltpu.VMEM((tokens, width), f32),
            pltpu.VMEM(x.shape, bf16),
            pltpu.VMEM(pm.shape, bf16),
            pltpu.VMEM((K, R, width), bf16),
            dma((7,)),
            dma((2,)),
            dma((4 * N, WINDOW)),
            dma((2 * N, K)),
            dma((4 * N,)),
            dma((2 * N,)),
            dma((T,)),
            dma((T,)),
            dma((T,)),
            dma((T,)),
            dma((T,)),
            dma((T,)),
            dma((E,)),
            dma((E,)),
            dma((2,)),
            dma((T,)),
            dma((T,)),
        ],
        compiler_params=pltpu.CompilerParams(
            collective_id=0, has_side_effects=True, vmem_limit_bytes=61 * 1024 * 1024
        ),
    )(x, cot, gate, up, w.reshape(K, R, w.shape[1]), pm, ph.reshape(K, R, width), q, lengths)


def per_device(
    N, T, inputs, cotangent, gate_pre, up_pre, w_down, proj_model, proj_hidden, queries, lengths
):
    rank = proj_model.shape[1] // 2
    routes = lengths.shape[0]
    features, query_rows = gather_and_project(
        N, T, inputs, cotangent, gate_pre, up_pre, w_down, proj_model, proj_hidden, queries, lengths
    )
    features = features.reshape(routes, rank, 2, rank).transpose(0, 2, 1, 3).reshape(routes, -1)
    return jnp.dot(features, query_rows.astype(jnp.float32).T, precision=lax.Precision.HIGHEST)


def solution(mesh):
    return jax.shard_map(
        functools.partial(per_device, mesh.shape["dp"] // 2, mesh.shape["tensor"]),
        mesh=mesh,
        in_specs=(
            P(("dp", "tensor"), None),
            P(("dp", "tensor"), None),
            P("dp", "tensor"),
            P("dp", "tensor"),
            P("tensor", "dp"),
            P(),
            P("tensor", None),
            P("tensor", "dp"),
            P("dp"),
        ),
        out_specs=P("dp", "tensor"),
        check_vma=False,
    )
```
